1024 devices in a mesh: dp: 128 (over z, x, core), node: 8 (over y).
Axes of the slice: x: 4, y: 8, z: 16, core: 2. Of those that a mesh axis runs over, the one named last changes fastest.
Arguments:
- tokens: bfloat16 [131072, 4096], P('dp', 'node'), may hold values from -24 to 24
- weight_codes: bfloat16 [4096, 1024], P(('node', 'dp')), may hold values from -127 to 127, as said below
- block_scales: bfloat16 [4096, 4], P(('node', 'dp')), may hold values from 4.9829483e-05 to 0.00049972534
- cotangent: bfloat16 [131072, 1024], P('dp', 'node'), may hold values from -6 to 6
Outputs:
- values: bfloat16 [131072, 1024], P('dp', 'node')
- token_grad: bfloat16 [131072, 4096], P('dp', 'node')
- weight_grad: float32 [4096, 1024], P(('node', 'dp'))
The draws below stay inside these ranges and needn't reach their ends.
Inputs may be any that keep to these rules, and one draw needn't show every extreme that they name: `weight_codes`: every entry is a whole number.
All inputs are finite; a program needn't handle non-finite values.
Results may differ from the reference program's by a relative error of at most 0.017.
Values may be sent and summed in bfloat16 or wider, within the bound.
A program may use at most 32 MiB of HBM per device.

```python
import math
import jax
import jax.numpy as jnp
from jax import lax

D = 4096
COLS = 1024
BLOCK = 256
TOKENS = 131072
N_NODE = 8


def draw_weight_codes(key, part):
    key = jax.random.fold_in(key, 11)
    whole = jax.random.randint(key, (D, COLS), -127, 128)
    return whole.astype(jnp.float32).astype(jnp.bfloat16)


def raised(values, rng, source, target, blocks, factor):
    def block_of(dim):
        return (jnp.arange(values.shape[dim]) // (values.shape[dim] // blocks)).reshape((-1,) + (1,) * (values.ndim - 1 - dim))

    near = jax.random.permutation(rng, blocks)[block_of(target)]
    far = (block_of(target) + blocks // 2) % blocks
    return jnp.where((block_of(source) == near) | (block_of(source) == far), factor * values, values)


def shard_levels(rng, extent, split, low, largest):
    def one(axis_at, shards_of):
        heights = jax.random.uniform(jax.random.fold_in(jax.random.fold_in(rng, 6), axis_at), (shards_of,), jnp.float32, low / len(split), largest / len(split))
        return jnp.repeat(jnp.exp(heights), extent[axis_at] // shards_of).reshape((-1,) + (1,) * (len(extent) - axis_at - 1))

    level = one(*split[0])
    for cut in split[1:]:
        level = level * one(*cut)
    return level


def noise(own_key, shape, deviation, reach, pieces=(), dtype=jnp.bfloat16):
    array = jax.random.normal(own_key, shape, jnp.float32) * deviation
    if len(pieces) > 0:
        array = shard_levels(own_key, shape, pieces, -0.22, 0.18) * array
    return jnp.clip(array, min=-reach, max=reach).astype(dtype)


def bell_draw_with(own_key, shape, scale, limit, split, heavy, held_as=jnp.bfloat16):
    drawn = scale * jax.random.normal(own_key, shape, jnp.float32)
    if split:
        drawn = drawn * shard_levels(own_key, shape, split, -0.22, 0.18)
    return jnp.clip(raised(drawn, jax.random.fold_in(own_key, 3), *heavy), -limit, limit).astype(held_as)


def setup_inputs(seed: int = 0) -> dict:
    key_of = jax.random.split(jax.random.key(seed), 5)
    return {
        "tokens": bell_draw_with(key_of[0], (TOKENS, D), 1.0, 24.0, ((0, 128), (1, 8)), (0, 1, 128, 5.5)),
        "weight_codes": draw_weight_codes(jax.random.fold_in(key_of[4], 71), 0),
        "block_scales": jnp.clip(jnp.exp(math.log(0.00049972534) - 2.3054518 * jax.random.uniform(key_of[2], (D, COLS // BLOCK), jnp.float32) ** shard_levels(key_of[2], (D, COLS // BLOCK), ((0, 1024),), -0.2, 0.2)), 4.982948303222656e-05, 0.00049972534).astype(jnp.bfloat16),
        "cotangent": noise(key_of[3], (TOKENS, COLS), 1.0, 6.0, ((0, 128), (1, 8))),
    }


def dequantize(code_rows, scales):
    blocks = scales.shape[1]
    grouped = code_rows.astype(jnp.float32).reshape(code_rows.shape[0], blocks, -1)
    scaled = grouped * scales.astype(jnp.float32)[:, :, None]
    return scaled.reshape(code_rows.shape).astype(jnp.bfloat16)

def reference(tokens, weight_codes, block_scales, cotangent):
    weight = dequantize(weight_codes, block_scales)
    slab_width = D // N_NODE
    summed = jnp.zeros((TOKENS, COLS), jnp.float32)
    for slab_index in range(N_NODE):
        lower = slab_index * slab_width
        partial_value = jnp.dot(tokens[:, lower:lower + slab_width], weight[lower:lower + slab_width], preferred_element_type=jnp.float32)
        rounded = lax.optimization_barrier(partial_value.astype(jnp.bfloat16))
        summed = summed + rounded.astype(jnp.float32)
    values = summed.astype(jnp.bfloat16)
    token_grad = lax.dot_general(cotangent, weight, (((1,), (1,)), ((), ())), preferred_element_type=jnp.float32).astype(jnp.bfloat16)
    weight_grad = lax.dot_general(tokens, cotangent, (((0,), (0,)), ((), ())), preferred_element_type=jnp.float32)
    weight_grad = weight_grad * jnp.float32(1.0 / math.sqrt(TOKENS))
    return (values, token_grad, weight_grad)
```

```python
import functools
import math

import jax
import jax.numpy as jnp
from jax import lax
from jax.experimental import pallas as pl
from jax.experimental.pallas import tpu as pltpu
from jax.sharding import PartitionSpec as P

NX = 4
PIECES = 4
BF16, F32 = jnp.bfloat16, jnp.float32
MESH = pl.DeviceIdType.MESH


def kernel(ny, nz, nx, tok_ref, code_ref, scale_ref, cot_ref,
           val_ref, tg_ref, wg_ref,
           tok, tok_t, codes, scales, full, gat, tmp, w, part, rss, rsr,
           vout, tgout, mine, sibs, sibr, xs, xr, zs, zr, fs, fr, wgout,
           in_sem, out_sem, ag_s, ag_r, rs_s, rs_r,
           wz_s, wz_r, wx_s, wx_r, wc_s, wc_r,
           gc_s, gc_r, gx_s, gx_r, gz_s, gz_r, gf_s, gf_r):
    rows, feats = tok.shape
    cols = codes.shape[1]
    hops = ny // 2
    piece = rows // PIECES
    half = PIECES // 2
    mb = ny // 4
    inv = 1.0 / math.sqrt(rows * nz * nx * 2)

    y = lax.axis_index("node")
    dp = lax.axis_index("dp")
    c = lax.rem(dp, 2)
    x = lax.rem(dp // 2, nx)
    z = dp // (2 * nx)

    def at(zz, xx, cc):
        return ((zz * nx + xx) * 2 + cc, y)

    right, left = (dp, lax.rem(y + 1, ny)), (dp, lax.rem(y + ny - 1, ny))
    sibling = at(z, x, 1 - c)

    def remote(src, dst, s_sem, r_sem, dev):
        return pltpu.make_async_remote_copy(
            src_ref=src, dst_ref=dst, send_sem=s_sem, recv_sem=r_sem, device_id=dev, device_id_type=MESH)

    def loop(n, body):
        lax.fori_loop(0, n, lambda i, carry: (body(i), carry)[1], 0)

    cp_cot = pltpu.make_async_copy(cot_ref, full.at[0], in_sem.at[0])
    cp_code = pltpu.make_async_copy(code_ref, codes, in_sem.at[1])
    cp_scale = pltpu.make_async_copy(scale_ref, scales, in_sem.at[2])
    cp_tok = pltpu.make_async_copy(tok_ref, tok, in_sem.at[3])
    for cp in (cp_cot, cp_code, cp_scale, cp_tok):
        cp.start()

    barrier = pltpu.get_barrier_semaphore()

    def greet(dev):
        pl.semaphore_signal(barrier, inc=1, device_id=dev, device_id_type=MESH)

    greet(right)
    greet(left)
    greet(sibling)
    for j in range(1, nx):
        greet(at(z, lax.rem(x + j, nx), c))
    loop(nz - 1, lambda j: greet(at(lax.rem(z + j + 1, nz), x, c)))
    pl.semaphore_wait(barrier, 3 + nx - 1 + nz - 1)

    def ag(d, h, p):
        src, dst = (h - 1, h) if d == 0 else ((ny - h + 1) % ny, ny - h)
        span = pl.ds(pl.multiple_of(p * piece, piece), piece)
        return remote(full.at[src, span], full.at[dst, span], ag_s.at[d, h - 1, p], ag_r.at[d, h - 1, p],
                      right if d == 0 else left)

    def ag_first():
        loop(PIECES, lambda p: (ag(0, 1, p).start(), ag(1, 1, p).start()))

    def ag_hop(h):
        if h == hops:
            loop(half, lambda p: (ag(0, h, p).wait_recv(), ag(1, h, p + half).wait_recv()))
        elif h == hops - 1:
            def body(p):
                q = p + half
                ag(0, h, p).wait_recv()
                ag(0, h + 1, p).start()
                ag(1, h, q).wait_recv()
                ag(1, h + 1, q).start()
            loop(half, body)
            loop(half, lambda p: (ag(0, h, p + half).wait_recv(), ag(1, h, p).wait_recv()))
        else:
            def body(p):
                ag(0, h, p).wait_recv()
                ag(0, h + 1, p).start()
                ag(1, h, p).wait_recv()
                ag(1, h + 1, p).start()
            loop(PIECES, body)

    def ag_drain():
        for h in range(1, hops):
            loop(PIECES, lambda p: (ag(0, h, p).wait_send(), ag(1, h, p).wait_send()))
        loop(half, lambda p: (ag(0, hops, p).wait_send(), ag(1, hops, p + half).wait_send()))

    def wz(j):
        return remote(gat.at[c, x, z], gat.at[c, x, z], wz_s.at[j], wz_r.at[j],
                      at(lax.rem(z + j + 1, nz), x, c))

    def wx(j):
        return remote(gat.at[c, x], gat.at[c, x], wx_s.at[j], wx_r.at[j], at(z, lax.rem(x + j + 1, nx), c))

    def wc(j):
        xx = lax.rem(x - j + nx, nx)
        return remote(gat.at[c, xx], gat.at[c, xx], wc_s.at[j], wc_r.at[j], sibling)

    def w_first():
        scale = scales[...].astype(F32)
        block = cols // scale.shape[1]
        for b in range(scale.shape[1]):
            span = slice(b * block, (b + 1) * block)
            gat[c, x, z, :, span] = (codes[:, span].astype(F32) * scale[:, b:b + 1]).astype(BF16)
        loop(nz - 1, lambda j: wz(j).start())

    def w_along_x():
        def arrived(j):
            zz = lax.rem(z + nz - j - 1, nz)
            remote(gat.at[c, x, zz], gat.at[c, x, zz], wz_s.at[j], wz_r.at[j], sibling).wait_recv()
        loop(nz - 1, arrived)
        for j in range(nx - 1):
            wx(j).start()
        wc(0).start()

    def w_across():
        for j in range(1, nx):
            xx = lax.rem(x + nx - j, nx)
            remote(gat.at[c, xx], gat.at[c, xx], wx_s.at[j - 1], wx_r.at[j - 1], sibling).wait_recv()
            wc(j).start()

    def w_done():
        for j in range(nx):
            xx = lax.rem(x + nx - j, nx)
            remote(gat.at[1 - c, xx], gat.at[1 - c, xx], wc_s.at[j], wc_r.at[j], sibling).wait_recv()

        def lay(zz):
            for xx in range(nx):
                for cc in range(2):
                    at_row = 8 * xx + 4 * cc
                    tmp[at_row:at_row + 4, :] = gat[cc, xx, zz].astype(F32)
            n = 8 * nx
            w[pl.ds(pl.multiple_of(zz * n, n), n), :] = tmp[...].astype(BF16)
        loop(nz, lay)

    def w_drain():
        loop(nz - 1, lambda j: wz(j).wait_send())
        for j in range(nx - 1):
            wx(j).wait_send()
        for j in range(nx):
            wc(j).wait_send()

    tile = min(256, piece)

    def w_cols(k):
        owner = lax.rem(y + k, ny)
        return w[:, pl.ds(pl.multiple_of(owner * 128, 128), 128)]

    def partial(*ks):
        def body(i):
            span = pl.ds(pl.multiple_of(i * tile, tile), tile)
            rhs = jnp.concatenate([w_cols(k) for k in ks], axis=1)
            out = jnp.dot(tok[span, :], rhs, preferred_element_type=F32)
            for n, k in enumerate(ks):
                part[k, span, :] = out[:, n * 128:(n + 1) * 128]
        loop(rows // tile, body)

    def rs(d, t, p):
        span = pl.ds(pl.multiple_of(p * piece, piece), piece)
        return remote(rss.at[d, t - 1, span], rsr.at[d, t - 1, span], rs_s.at[d, t - 1, p], rs_r.at[d, t - 1, p],
                      right if d == 0 else left)

    def rs_send(d, t, p, arrives):
        s = hops - t + 1
        k = s if d == 0 else ny - s
        span = pl.ds(pl.multiple_of(p * piece, piece), piece)
        total = part[k, span, :]
        if arrives:
            rs(d, t - 1, p).wait_recv()
            total = total + rsr[d, t - 2, span, :].astype(F32)
        rss[d, t - 1, span, :] = total.astype(BF16)
        rs(d, t, p).start()

    def rs_first():
        loop(half, lambda p: (rs_send(0, 1, p, False), rs_send(1, 1, p + half, False)))

    def rs_second_own():
        loop(half, lambda p: (rs_send(0, 2, p + half, False), rs_send(1, 2, p, False)))

    def rs_second_sum():
        loop(half, lambda p: (rs_send(0, 2, p, True), rs_send(1, 2, p + half, True)))

    def rs_step(t, lo=0, hi=PIECES):
        def body(i):
            p = i + lo
            rs_send(0, t, lax.rem(p + half, PIECES), True)
            rs_send(1, t, p, True)
        loop(hi - lo, body)

    def rs_out(p):
        span = pl.ds(pl.multiple_of(p * piece, piece), piece)
        return pltpu.make_async_copy(vout.at[span], val_ref.at[span], out_sem.at[p])

    def rs_last():
        def body(i):
            rs(0, hops, lax.rem(i + half, PIECES)).wait_recv()
            rs(1, hops, i).wait_recv()
        loop(half, body)

        def fin(i):
            a, b = i, i + half
            rs(0, hops, a).wait_recv()
            rs(1, hops, b).wait_recv()
            for p in (a, b):
                span = pl.ds(pl.multiple_of(p * piece, piece), piece)
                total = part[0, span, :] + rsr[0, hops - 1, span, :].astype(F32) + rsr[1, hops - 1, span, :].astype(F32)
                vout[span, :] = total.astype(BF16)
                rs_out(p).start()
        loop(half, fin)

    def rs_drain():
        loop(half, lambda p: (rs(0, 1, p).wait_send(), rs(1, 1, p + half).wait_send()))
        for t in range(2, hops + 1):
            loop(PIECES, lambda p: (rs(0, t, p).wait_send(), rs(1, t, p).wait_send()))

    def token_grad(lo, hi):
        def body(i):
            span = pl.ds(pl.multiple_of((i + lo) * tile, tile), tile)
            lhs = jnp.concatenate([full[lax.rem(y + ny - k, ny), span, :] for k in range(ny)], axis=1)
            out = lax.dot_general(lhs, w[...], (((1,), (1,)), ((), ())), preferred_element_type=F32)
            tgout[span, :] = out.astype(BF16)
        loop(hi - lo, body)

    cp_tg = pltpu.make_async_copy(tgout, tg_ref, out_sem.at[PIECES])

    order = [0]
    for k in range(1, hops):
        order += [k, ny - k]
    order.append(hops)

    def slots(ph, cc):
        first = order[ph * 2 * mb:ph * 2 * mb + mb]
        second = order[ph * 2 * mb + mb:(ph + 1) * 2 * mb]
        return [jnp.where(cc == 0, a, b) for a, b in zip(first, second)]

    def wg_term(ph, cc, out):
        group = min(128, feats)
        per = group // (8 * nx)

        def body(i):
            rhs = jnp.concatenate([full[s] for s in slots(ph, cc)], axis=1)
            term = jnp.dot(tok_t[pl.ds(pl.multiple_of(i * group, group), group), :], rhs, preferred_element_type=F32)
            for u in range(per):
                for xx in range(nx):
                    for m in range(mb):
                        lo = (u * nx + xx) * 8
                        out[ph, xx, i * per + u, m] = term[lo:lo + 8, m * 128:(m + 1) * 128].astype(out.dtype)
        loop(feats // group, body)

    def gc(ph):
        return remote(sibs.at[ph], sibr.at[ph], gc_s.at[ph], gc_r.at[ph], sibling)

    def gx(ph, j):
        return remote(xs.at[ph, j], xr.at[ph, j], gx_s.at[ph, j], gx_r.at[ph, j], at(z, lax.rem(x + j + 1, nx), c))

    def gz(ph, j):
        zz = lax.rem(z + j + 1, nz)
        return remote(zs.at[ph, zz], zr.at[ph, j], gz_s.at[ph, j], gz_r.at[ph, j], at(zz, x, c))

    def gf(ph):
        return remote(fs.at[ph], fr.at[ph], gf_s.at[ph], gf_r.at[ph], sibling)

    def wg_first(ph):
        wg_term(ph, 1 - c, sibs)
        gc(ph).start()
        wg_term(ph, c, mine)

    def wg_along_x(ph):
        gc(ph).wait_recv()

        def body(zz):
            for j in range(nx):
                xx = lax.rem(x + j, nx)
                total = mine[ph, xx, zz] + sibr[ph, xx, zz].astype(F32)
                if j == 0:
                    mine[ph, xx, zz] = total
                else:
                    xs[ph, j - 1, zz] = total.astype(BF16)
        loop(nz, body)
        for j in range(nx - 1):
            gx(ph, j).start()

    def wg_along_z(ph):
        for j in range(nx - 1):
            gx(ph, j).wait_recv()

        def body(zz):
            total = mine[ph, x, zz]
            for j in range(nx - 1):
                total = total + xr[ph, j, zz].astype(F32)
            mine[ph, x, zz] = total
            zs[ph, zz] = total.astype(BF16)
        loop(nz, body)
        loop(nz - 1, lambda j: gz(ph, j).start())

    def place(ph, cc, value):
        for m, s in enumerate(slots(ph, cc)):
            col = lax.rem(y + ny - s, ny) * 128
            wgout[:, pl.ds(pl.multiple_of(col, 128), 128)] = value[m]

    def wg_across(ph):
        loop(nz - 1, lambda j: gz(ph, j).wait_recv())
        total = mine[ph, x, z]
        for j in range(nz - 1):
            total = total + zr[ph, j].astype(F32)
        total = total * F32(inv)
        low, high = total[:, :4, :], total[:, 4:, :]
        fs[ph] = jnp.where(c == 0, high, low)
        gf(ph).start()
        place(ph, c, jnp.where(c == 0, low, high))

    cp_wg = pltpu.make_async_copy(wgout, wg_ref, out_sem.at[PIECES + 1])

    def wg_last():
        for ph in range(2):
            gf(ph).wait_recv()
            place(ph, 1 - c, fr[ph])
        cp_wg.start()

    def wg_drain():
        for ph in range(2):
            gc(ph).wait_send()
            for j in range(nx - 1):
                gx(ph, j).wait_send()
            loop(nz - 1, lambda j: gz(ph, j).wait_send())
            gf(ph).wait_send()

    def turn():
        step = min(256, rows)

        def body(i):
            span = pl.ds(pl.multiple_of(i * step, step), step)
            tok_t[:, span] = tok[span, :].T
        loop(rows // step, body)

    cp_cot.wait()
    ag_first()
    cp_code.wait()
    cp_scale.wait()
    w_first()
    cp_tok.wait()
    turn()
    ag_hop(1)
    w_along_x()
    for h in range(2, hops - 1):
        ag_hop(h)
    w_across()
    wg_first(0)
    ag_hop(hops - 1)
    wg_along_x(0)
    w_done()
    partial(hops)
    rs_first()
    ag_hop(hops)
    partial(hops - 1, hops + 1)
    rs_second_own()
    wg_along_z(0)
    wg_first(1)
    for k in range(hops - 2, 0, -1):
        partial(k, ny - k)
    rs_second_sum()
    wg_along_x(1)
    partial(0)
    wg_across(0)
    if hops > 2:
        rs_step(3)
    wg_along_z(1)
    token_grad(0, rows // tile // 2)
    for t in range(4, hops + 1):
        rs_step(t)
    wg_across(1)
    token_grad(rows // tile // 2, rows // tile)
    cp_tg.start()
    wg_last()
    rs_last()
    ag_drain()
    w_drain()
    wg_drain()
    rs_drain()
    loop(PIECES, lambda p: rs_out(p).wait())
    cp_tg.wait()
    cp_wg.wait()


def on_device(ny, nz, nx, tokens, codes, scales, cot):
    rows, feats = tokens.shape
    cols = codes.shape[1]
    hops, mb = ny // 2, ny // 4
    any_ = pl.BlockSpec(memory_space=pl.ANY)
    dma = pltpu.SemaphoreType.DMA
    v = pltpu.VMEM
    scratch = [
        v((rows, feats), BF16), v((feats, rows), BF16), v(codes.shape, BF16), v(scales.shape, BF16),
        v((ny, rows, 128), BF16), v((2, nx, nz, 4, cols), BF16), v((8 * nx, cols), F32), v((feats, cols), BF16),
        v((ny, rows, 128), F32), v((2, hops, rows, 128), BF16), v((2, hops, rows, 128), BF16),
        v((rows, 128), BF16), v((rows, feats), BF16),
        v((2, nx, nz, mb, 8, 128), F32), v((2, nx, nz, mb, 8, 128), BF16), v((2, nx, nz, mb, 8, 128), BF16),
        v((2, nx - 1, nz, mb, 8, 128), BF16), v((2, nx - 1, nz, mb, 8, 128), BF16),
        v((2, nz, mb, 8, 128), BF16), v((2, nz - 1, mb, 8, 128), BF16),
        v((2, mb, 4, 128), F32), v((2, mb, 4, 128), F32), v((4, cols), F32),
        dma((4,)), dma((PIECES + 2,)),
        dma((2, hops, PIECES)), dma((2, hops, PIECES)), dma((2, hops, PIECES)), dma((2, hops, PIECES)),
        dma((nz - 1,)), dma((nz - 1,)), dma((nx - 1,)), dma((nx - 1,)), dma((nx,)), dma((nx,)),
        dma((2,)), dma((2,)), dma((2, nx - 1)), dma((2, nx - 1)), dma((2, nz - 1)), dma((2, nz - 1)),
        dma((2,)), dma((2,)),
    ]
    flops = 6 * rows * feats * cols
    return pl.pallas_call(
        functools.partial(kernel, ny, nz, nx),
        out_shape=(
            jax.ShapeDtypeStruct((rows, 128), BF16),
            jax.ShapeDtypeStruct((rows, feats), BF16),
            jax.ShapeDtypeStruct((4, cols), F32),
        ),
        in_specs=[any_] * 4,
        out_specs=(any_,) * 3,
        scratch_shapes=scratch,
        compiler_params=pltpu.CompilerParams(
            collective_id=0, has_side_effects=True, vmem_limit_bytes=56 * 2**20),
        cost_estimate=pl.CostEstimate(flops=flops, bytes_accessed=4 * rows * feats, transcendentals=0),
    )(tokens, codes, scales, cot)


def build(mesh, nx):
    ny = mesh.shape["node"]
    nz = mesh.shape["dp"] // (2 * nx)
    placed = (P("dp", "node"), P(("node", "dp"), None), P(("node", "dp"), None), P("dp", "node"))
    return jax.shard_map(
        functools.partial(on_device, ny, nz, nx),
        mesh=mesh,
        in_specs=placed,
        out_specs=(P("dp", "node"), P("dp", "node"), P(("node", "dp"), None)),
        check_vma=False,
    )


def solution(mesh):
    return build(mesh, NX)
```

```python
import functools
import math

import jax
import jax.numpy as jnp
from jax import lax
from jax.experimental import pallas as pl
from jax.experimental.pallas import tpu as pltpu
from jax.sharding import PartitionSpec as P

NX = 4
PIECES = 4
BF16, F32 = jnp.bfloat16, jnp.float32
MESH = pl.DeviceIdType.MESH


def kernel(ny, nz, nx, tok_ref, code_ref, scale_ref, cot_ref,
           vout, tgout, wgout,
           tok, tok_t, codes, scales, full, gat, tmp, w, part, rss, rsr,
           mine, sibs, sibr, xs, xr, zs, zr, fs, fr,
           in_sem, ag_s, ag_r, rs_s, rs_r,
           wz_s, wz_r, wx_s, wx_r, wc_s, wc_r,
           gc_s, gc_r, gx_s, gx_r, gz_s, gz_r, gf_s, gf_r):
    rows, feats = tok.shape
    cols = codes.shape[1]
    hops = ny // 2
    piece = rows // PIECES
    half = PIECES // 2
    mb = ny // 4
    inv = 1.0 / math.sqrt(rows * nz * nx * 2)

    y = lax.axis_index("node")
    dp = lax.axis_index("dp")
    c = lax.rem(dp, 2)
    x = lax.rem(dp // 2, nx)
    z = dp // (2 * nx)

    def at(zz, xx, cc):
        return ((zz * nx + xx) * 2 + cc, y)

    right, left = (dp, lax.rem(y + 1, ny)), (dp, lax.rem(y + ny - 1, ny))
    sibling = at(z, x, 1 - c)

    def remote(src, dst, s_sem, r_sem, dev):
        return pltpu.make_async_remote_copy(
            src_ref=src, dst_ref=dst, send_sem=s_sem, recv_sem=r_sem, device_id=dev, device_id_type=MESH)

    def loop(n, body):
        lax.fori_loop(0, n, lambda i, carry: (body(i), carry)[1], 0)

    cp_cot = pltpu.make_async_copy(cot_ref, full.at[0], in_sem.at[0])
    cp_code = pltpu.make_async_copy(code_ref, codes, in_sem.at[1])
    cp_scale = pltpu.make_async_copy(scale_ref, scales, in_sem.at[2])
    cp_tok = pltpu.make_async_copy(tok_ref, tok, in_sem.at[3])
    for cp in (cp_cot, cp_code, cp_scale, cp_tok):
        cp.start()

    barrier = pltpu.get_barrier_semaphore()

    def greet(dev):
        pl.semaphore_signal(barrier, inc=1, device_id=dev, device_id_type=MESH)

    greet(right)
    greet(left)
    greet(sibling)
    for j in range(1, nx):
        greet(at(z, lax.rem(x + j, nx), c))
    loop(nz - 1, lambda j: greet(at(lax.rem(z + j + 1, nz), x, c)))
    pl.semaphore_wait(barrier, 3 + nx - 1 + nz - 1)

    def ag(d, h, p):
        src, dst = (h - 1, h) if d == 0 else ((ny - h + 1) % ny, ny - h)
        span = pl.ds(pl.multiple_of(p * piece, piece), piece)
        return remote(full.at[src, span], full.at[dst, span], ag_s.at[d, h - 1, p], ag_r.at[d, h - 1, p],
                      right if d == 0 else left)

    def ag_first():
        loop(PIECES, lambda p: (ag(0, 1, p).start(), ag(1, 1, p).start()))

    def ag_hop(h):
        if h == hops:
            loop(half, lambda p: (ag(0, h, p).wait_recv(), ag(1, h, p + half).wait_recv()))
        elif h == hops - 1:
            def body(p):
                q = p + half
                ag(0, h, p).wait_recv()
                ag(0, h + 1, p).start()
                ag(1, h, q).wait_recv()
                ag(1, h + 1, q).start()
            loop(half, body)
            loop(half, lambda p: (ag(0, h, p + half).wait_recv(), ag(1, h, p).wait_recv()))
        else:
            def body(p):
                ag(0, h, p).wait_recv()
                ag(0, h + 1, p).start()
                ag(1, h, p).wait_recv()
                ag(1, h + 1, p).start()
            loop(PIECES, body)

    def ag_drain():
        for h in range(1, hops):
            loop(PIECES, lambda p: (ag(0, h, p).wait_send(), ag(1, h, p).wait_send()))
        loop(half, lambda p: (ag(0, hops, p).wait_send(), ag(1, hops, p + half).wait_send()))

    def wz(j):
        return remote(gat.at[c, x, z], gat.at[c, x, z], wz_s.at[j], wz_r.at[j],
                      at(lax.rem(z + j + 1, nz), x, c))

    def wx(j):
        return remote(gat.at[c, x], gat.at[c, x], wx_s.at[j], wx_r.at[j], at(z, lax.rem(x + j + 1, nx), c))

    def wc(j):
        xx = lax.rem(x - j + nx, nx)
        return remote(gat.at[c, xx], gat.at[c, xx], wc_s.at[j], wc_r.at[j], sibling)

    def w_first():
        scale = scales[...].astype(F32)
        block = cols // scale.shape[1]
        for b in range(scale.shape[1]):
            span = slice(b * block, (b + 1) * block)
            gat[c, x, z, :, span] = (codes[:, span].astype(F32) * scale[:, b:b + 1]).astype(BF16)
        loop(nz - 1, lambda j: wz(j).start())

    def w_along_x():
        def arrived(j):
            zz = lax.rem(z + nz - j - 1, nz)
            remote(gat.at[c, x, zz], gat.at[c, x, zz], wz_s.at[j], wz_r.at[j], sibling).wait_recv()
        loop(nz - 1, arrived)
        for j in range(nx - 1):
            wx(j).start()
        wc(0).start()

    def w_across():
        for j in range(1, nx):
            xx = lax.rem(x + nx - j, nx)
            remote(gat.at[c, xx], gat.at[c, xx], wx_s.at[j - 1], wx_r.at[j - 1], sibling).wait_recv()
            wc(j).start()

    def w_done():
        for j in range(nx):
            xx = lax.rem(x + nx - j, nx)
            remote(gat.at[1 - c, xx], gat.at[1 - c, xx], wc_s.at[j], wc_r.at[j], sibling).wait_recv()

        def lay(zz):
            for xx in range(nx):
                for cc in range(2):
                    at_row = 8 * xx + 4 * cc
                    tmp[at_row:at_row + 4, :] = gat[cc, xx, zz].astype(F32)
            n = 8 * nx
            w[pl.ds(pl.multiple_of(zz * n, n), n), :] = tmp[...].astype(BF16)
        loop(nz, lay)

    def w_drain():
        loop(nz - 1, lambda j: wz(j).wait_send())
        for j in range(nx - 1):
            wx(j).wait_send()
        for j in range(nx):
            wc(j).wait_send()

    tile = min(256, piece)

    def w_cols(k):
        owner = lax.rem(y + k, ny)
        return w[:, pl.ds(pl.multiple_of(owner * 128, 128), 128)]

    def partial(*ks):
        def body(i):
            span = pl.ds(pl.multiple_of(i * tile, tile), tile)
            rhs = jnp.concatenate([w_cols(k) for k in ks], axis=1)
            out = jnp.dot(tok[span, :], rhs, preferred_element_type=F32)
            for n, k in enumerate(ks):
                part[k, span, :] = out[:, n * 128:(n + 1) * 128]
        loop(rows // tile, body)

    def rs(d, t, p):
        span = pl.ds(pl.multiple_of(p * piece, piece), piece)
        return remote(rss.at[d, t - 1, span], rsr.at[d, t - 1, span], rs_s.at[d, t - 1, p], rs_r.at[d, t - 1, p],
                      right if d == 0 else left)

    def rs_send(d, t, p, arrives):
        s = hops - t + 1
        k = s if d == 0 else ny - s
        span = pl.ds(pl.multiple_of(p * piece, piece), piece)
        total = part[k, span, :]
        if arrives:
            rs(d, t - 1, p).wait_recv()
            total = total + rsr[d, t - 2, span, :].astype(F32)
        rss[d, t - 1, span, :] = total.astype(BF16)
        rs(d, t, p).start()

    def rs_first():
        loop(half, lambda p: (rs_send(0, 1, p, False), rs_send(1, 1, p + half, False)))

    def rs_second_own():
        loop(half, lambda p: (rs_send(0, 2, p + half, False), rs_send(1, 2, p, False)))

    def rs_second_sum():
        loop(half, lambda p: (rs_send(0, 2, p, True), rs_send(1, 2, p + half, True)))

    def rs_step(t, late):
        def body(i):
            rs_send(0, t, i + (0 if late else half), True)
            rs_send(1, t, i + (half if late else 0), True)
        loop(half, body)

    def rs_last():
        def seen(i):
            rs(0, hops, i + half).wait_recv()
            rs(1, hops, i).wait_recv()
        loop(half, seen)

        def fin(i):
            a, b = i, i + half
            rs(0, hops, a).wait_recv()
            rs(1, hops, b).wait_recv()
            for p in (a, b):
                span = pl.ds(pl.multiple_of(p * piece, piece), piece)
                total = part[0, span, :] + rsr[0, hops - 1, span, :].astype(F32) + rsr[1, hops - 1, span, :].astype(F32)
                vout[span, :] = total.astype(BF16)
        loop(half, fin)

    def rs_drain():
        loop(half, lambda p: (rs(0, 1, p).wait_send(), rs(1, 1, p + half).wait_send()))
        for t in range(2, hops + 1):
            loop(PIECES, lambda p: (rs(0, t, p).wait_send(), rs(1, t, p).wait_send()))

    def token_grad(lo, hi):
        def body(i):
            span = pl.ds(pl.multiple_of((i + lo) * tile, tile), tile)
            lhs = jnp.concatenate([full[lax.rem(y + ny - k, ny), span, :] for k in range(ny)], axis=1)
            out = lax.dot_general(lhs, w[...], (((1,), (1,)), ((), ())), preferred_element_type=F32)
            tgout[span, :] = out.astype(BF16)
        loop(hi - lo, body)

    order = [0]
    for k in range(1, hops):
        order += [k, ny - k]
    order.append(hops)

    def slots(ph, cc):
        first = order[ph * 2 * mb:ph * 2 * mb + mb]
        second = order[ph * 2 * mb + mb:(ph + 1) * 2 * mb]
        return [jnp.where(cc == 0, a, b) for a, b in zip(first, second)]

    def wg_term(ph, cc, out):
        group = min(128, feats)
        per = group // (8 * nx)

        def body(i):
            rhs = jnp.concatenate([full[s] for s in slots(ph, cc)], axis=1)
            term = jnp.dot(tok_t[pl.ds(pl.multiple_of(i * group, group), group), :], rhs, preferred_element_type=F32)
            for u in range(per):
                for xx in range(nx):
                    for m in range(mb):
                        lo = (u * nx + xx) * 8
                        out[ph, xx, i * per + u, m] = term[lo:lo + 8, m * 128:(m + 1) * 128].astype(out.dtype)
        loop(feats // group, body)

    def gc(ph):
        return remote(sibs.at[ph], sibr.at[ph], gc_s.at[ph], gc_r.at[ph], sibling)

    def gx(ph, j):
        return remote(xs.at[ph, j], xr.at[ph, j], gx_s.at[ph, j], gx_r.at[ph, j], at(z, lax.rem(x + j + 1, nx), c))

    def gz(ph, j):
        zz = lax.rem(z + j + 1, nz)
        return remote(zs.at[ph, zz], zr.at[ph, j], gz_s.at[ph, j], gz_r.at[ph, j], at(zz, x, c))

    def gf(ph):
        return remote(fs.at[ph], fr.at[ph], gf_s.at[ph], gf_r.at[ph], sibling)

    def wg_theirs(ph):
        wg_term(ph, 1 - c, sibs)
        gc(ph).start()

    def wg_mine(ph):
        wg_term(ph, c, mine)

    def wg_along_x(ph):
        gc(ph).wait_recv()

        def body(zz):
            for j in range(nx):
                xx = lax.rem(x + j, nx)
                total = mine[ph, xx, zz] + sibr[ph, xx, zz].astype(F32)
                if j == 0:
                    mine[ph, xx, zz] = total
                else:
                    xs[ph, j - 1, zz] = total.astype(BF16)
        loop(nz, body)
        for j in range(nx - 1):
            gx(ph, j).start()

    def wg_along_z(ph):
        for j in range(nx - 1):
            gx(ph, j).wait_recv()

        def body(zz):
            total = mine[ph, x, zz]
            for j in range(nx - 1):
                total = total + xr[ph, j, zz].astype(F32)
            mine[ph, x, zz] = total
            zs[ph, zz] = total.astype(BF16)
        loop(nz, body)
        loop(nz - 1, lambda j: gz(ph, j).start())

    def place(ph, cc, value):
        for m, s in enumerate(slots(ph, cc)):
            col = lax.rem(y + ny - s, ny) * 128
            wgout[:, pl.ds(pl.multiple_of(col, 128), 128)] = value[m]

    def wg_across(ph):
        loop(nz - 1, lambda j: gz(ph, j).wait_recv())
        total = mine[ph, x, z]
        for j in range(nz - 1):
            total = total + zr[ph, j].astype(F32)
        total = total * F32(inv)
        low, high = total[:, :4, :], total[:, 4:, :]
        fs[ph] = jnp.where(c == 0, high, low)
        gf(ph).start()
        place(ph, c, jnp.where(c == 0, low, high))

    def wg_last():
        for ph in range(2):
            gf(ph).wait_recv()
            place(ph, 1 - c, fr[ph])

    def wg_drain():
        for ph in range(2):
            gc(ph).wait_send()
            for j in range(nx - 1):
                gx(ph, j).wait_send()
            loop(nz - 1, lambda j: gz(ph, j).wait_send())
            gf(ph).wait_send()

    def turn():
        step = min(256, rows)

        def body(i):
            span = pl.ds(pl.multiple_of(i * step, step), step)
            tok_t[:, span] = tok[span, :].T
        loop(rows // step, body)

    cp_cot.wait()
    ag_first()
    cp_code.wait()
    cp_scale.wait()
    w_first()
    cp_tok.wait()
    turn()
    ag_hop(1)
    w_along_x()
    for h in range(2, hops - 1):
        ag_hop(h)
    wg_theirs(0)
    wg_mine(0)
    w_across()
    ag_hop(hops - 1)
    wg_along_x(0)
    w_done()
    partial(hops)
    rs_first()
    ag_hop(hops)
    partial(hops - 1, hops + 1)
    rs_second_own()
    wg_theirs(1)
    wg_along_z(0)
    rs_second_sum()
    wg_mine(1)
    partial(2, ny - 2)
    wg_along_x(1)
    rs_step(3, False)
    partial(1, ny - 1)
    wg_across(0)
    rs_step(3, True)
    wg_along_z(1)
    rs_step(4, False)
    partial(0)
    token_grad(0, rows // tile // 2)
    rs_step(4, True)
    token_grad(rows // tile // 2, rows // tile)
    rs_last()
    wg_across(1)
    wg_last()
    ag_drain()
    w_drain()
    wg_drain()
    rs_drain()


def on_device(ny, nz, nx, tokens, codes, scales, cot):
    rows, feats = tokens.shape
    cols = codes.shape[1]
    hops, mb = ny // 2, ny // 4
    hbm = pl.BlockSpec(memory_space=pltpu.HBM)
    dma = pltpu.SemaphoreType.DMA
    v = pltpu.VMEM
    scratch = [
        v((rows, feats), BF16), v((feats, rows), BF16), v(codes.shape, BF16), v(scales.shape, BF16),
        v((ny, rows, 128), BF16), v((2, nx, nz, 4, cols), BF16), v((8 * nx, cols), F32), v((feats, cols), BF16),
        v((ny, rows, 128), F32), v((2, hops, rows, 128), BF16), v((2, hops, rows, 128), BF16),
        v((2, nx, nz, mb, 8, 128), F32), v((2, nx, nz, mb, 8, 128), BF16), v((2, nx, nz, mb, 8, 128), BF16),
        v((2, nx - 1, nz, mb, 8, 128), BF16), v((2, nx - 1, nz, mb, 8, 128), BF16),
        v((2, nz, mb, 8, 128), BF16), v((2, nz - 1, mb, 8, 128), BF16),
        v((2, mb, 4, 128), F32), v((2, mb, 4, 128), F32),
        dma((4,)),
        dma((2, hops, PIECES)), dma((2, hops, PIECES)), dma((2, hops, PIECES)), dma((2, hops, PIECES)),
        dma((nz - 1,)), dma((nz - 1,)), dma((nx - 1,)), dma((nx - 1,)), dma((nx,)), dma((nx,)),
        dma((2,)), dma((2,)), dma((2, nx - 1)), dma((2, nx - 1)), dma((2, nz - 1)), dma((2, nz - 1)),
        dma((2,)), dma((2,)),
    ]
    flops = 6 * rows * feats * cols
    shapes = (((rows, 128), BF16), ((rows, feats), BF16), ((4, cols), F32))
    return pl.pallas_call(
        functools.partial(kernel, ny, nz, nx),
        out_shape=tuple(v(shape, dtype) for shape, dtype in shapes),
        in_specs=[hbm] * 4,
        out_specs=(pl.BlockSpec(memory_space=v),) * 3,
        scratch_shapes=scratch,
        compiler_params=pltpu.CompilerParams(
            collective_id=0, has_side_effects=True, vmem_limit_bytes=61 * 2**20),
        cost_estimate=pl.CostEstimate(flops=flops, bytes_accessed=4 * rows * feats, transcendentals=0),
    )(tokens, codes, scales, cot)

def build(mesh, nx):
    ny = mesh.shape["node"]
    nz = mesh.shape["dp"] // (2 * nx)
    placed = (P("dp", "node"), P(("node", "dp"), None), P(("node", "dp"), None), P("dp", "node"))
    return jax.shard_map(
        functools.partial(on_device, ny, nz, nx),
        mesh=mesh,
        in_specs=placed,
        out_specs=(P("dp", "node"), P("dp", "node"), P(("node", "dp"), None)),
        check_vma=False,
    )


def solution(mesh):
    return build(mesh, NX)
```

```python
import functools
import math

import jax
import jax.numpy as jnp
from jax import lax
from jax.experimental import pallas as pl
from jax.experimental.pallas import tpu as pltpu
from jax.sharding import PartitionSpec as P

NX = 4
PIECES = 4
BF16, F32 = jnp.bfloat16, jnp.float32
MESH = pl.DeviceIdType.MESH


def phases(ny):
    return ny // 4, ny // 4


def kernel(ny, nz, nx, tok_ref, code_ref, scale_ref, cot_ref,
           vout, tgout, wgout,
           tok, tok_t, codes, scales, full, gat, tmp, w, part, rss, rsr,
           mine0, sibs0, sibr0, xs0, xr0, zs0, zr0, fs0, fr0, mine1, sibs1, sibr1, xs1, xr1, zs1, zr1, fs1, fr1,
           in_sem, ag_s, ag_r, rs_s, rs_r,
           wz_s, wz_r, wx_s, wx_r, wc_s, wc_r,
           gc_s, gc_r, gx_s, gx_r, gz_s, gz_r, gf_s, gf_r):
    rows, feats = tok.shape
    cols = codes.shape[1]
    hops = ny // 2
    piece = rows // PIECES
    half = PIECES // 2
    sizes = phases(ny)
    mine, sibs, sibr, xs, xr = (mine0, mine1), (sibs0, sibs1), (sibr0, sibr1), (xs0, xs1), (xr0, xr1)
    zs, zr, fs, fr = (zs0, zs1), (zr0, zr1), (fs0, fs1), (fr0, fr1)
    inv = 1.0 / math.sqrt(rows * nz * nx * 2)

    y = lax.axis_index("node")
    dp = lax.axis_index("dp")
    c = lax.rem(dp, 2)
    x = lax.rem(dp // 2, nx)
    z = dp // (2 * nx)

    def at(zz, xx, cc):
        return ((zz * nx + xx) * 2 + cc, y)

    right, left = (dp, lax.rem(y + 1, ny)), (dp, lax.rem(y + ny - 1, ny))
    sibling = at(z, x, 1 - c)

    def remote(src, dst, s_sem, r_sem, dev):
        return pltpu.make_async_remote_copy(
            src_ref=src, dst_ref=dst, send_sem=s_sem, recv_sem=r_sem, device_id=dev, device_id_type=MESH)

    def loop(n, body):
        lax.fori_loop(0, n, lambda i, carry: (body(i), carry)[1], 0)

    def far_first(body):
        def one(k):
            near = (k + 1) // 2
            body(nz // 2 - 1 + jnp.where(lax.rem(k, 2) == 0, near, -near))
        loop(nz - 1, one)

    cp_cot = pltpu.make_async_copy(cot_ref, full.at[0], in_sem.at[0])
    cp_code = pltpu.make_async_copy(code_ref, codes, in_sem.at[1])
    cp_scale = pltpu.make_async_copy(scale_ref, scales, in_sem.at[2])
    cp_tok = pltpu.make_async_copy(tok_ref, tok, in_sem.at[3])
    for cp in (cp_cot, cp_code, cp_scale, cp_tok):
        cp.start()

    barrier = pltpu.get_barrier_semaphore()

    def greet(dev):
        pl.semaphore_signal(barrier, inc=1, device_id=dev, device_id_type=MESH)

    greet(right)
    greet(left)
    greet(sibling)
    for j in range(1, nx):
        greet(at(z, lax.rem(x + j, nx), c))
    far_first(lambda j: greet(at(lax.rem(z + j + 1, nz), x, c)))
    pl.semaphore_wait(barrier, 3 + nx - 1 + nz - 1)

    def ag(d, h, p):
        src, dst = (h - 1, h) if d == 0 else ((ny - h + 1) % ny, ny - h)
        span = pl.ds(pl.multiple_of(p * piece, piece), piece)
        return remote(full.at[src, span], full.at[dst, span], ag_s.at[d, h - 1, p], ag_r.at[d, h - 1, p],
                      right if d == 0 else left)

    def ag_first():
        loop(PIECES, lambda p: (ag(0, 1, p).start(), ag(1, 1, p).start()))

    def ag_hop(h):
        if h == hops:
            loop(half, lambda p: (ag(0, h, p).wait_recv(), ag(1, h, p + half).wait_recv()))
        elif h == hops - 1:
            def body(p):
                q = p + half
                ag(0, h, p).wait_recv()
                ag(0, h + 1, p).start()
                ag(1, h, q).wait_recv()
                ag(1, h + 1, q).start()
            loop(half, body)
            loop(half, lambda p: (ag(0, h, p + half).wait_recv(), ag(1, h, p).wait_recv()))
        else:
            def body(p):
                ag(0, h, p).wait_recv()
                ag(0, h + 1, p).start()
                ag(1, h, p).wait_recv()
                ag(1, h + 1, p).start()
            loop(PIECES, body)

    def ag_drain():
        for h in range(1, hops):
            loop(PIECES, lambda p: (ag(0, h, p).wait_send(), ag(1, h, p).wait_send()))
        loop(half, lambda p: (ag(0, hops, p).wait_send(), ag(1, hops, p + half).wait_send()))

    def wz(j):
        return remote(gat.at[c, x, z], gat.at[c, x, z], wz_s.at[j], wz_r.at[j],
                      at(lax.rem(z + j + 1, nz), x, c))

    def wx(j):
        return remote(gat.at[c, x], gat.at[c, x], wx_s.at[j], wx_r.at[j], at(z, lax.rem(x + j + 1, nx), c))

    def wc(j):
        xx = lax.rem(x - j + nx, nx)
        return remote(gat.at[c, xx], gat.at[c, xx], wc_s.at[j], wc_r.at[j], sibling)

    def w_first():
        scale = scales[...].astype(F32)
        block = cols // scale.shape[1]
        for b in range(scale.shape[1]):
            span = slice(b * block, (b + 1) * block)
            gat[c, x, z, :, span] = (codes[:, span].astype(F32) * scale[:, b:b + 1]).astype(BF16)
        far_first(lambda j: wz(j).start())

    def w_along_x():
        def arrived(j):
            zz = lax.rem(z + nz - j - 1, nz)
            remote(gat.at[c, x, zz], gat.at[c, x, zz], wz_s.at[j], wz_r.at[j], sibling).wait_recv()
        loop(nz - 1, arrived)
        for j in range(nx - 1):
            wx(j).start()
        wc(0).start()

    def w_across():
        for j in range(1, nx):
            xx = lax.rem(x + nx - j, nx)
            remote(gat.at[c, xx], gat.at[c, xx], wx_s.at[j - 1], wx_r.at[j - 1], sibling).wait_recv()
            wc(j).start()

    def w_done():
        for j in range(nx):
            xx = lax.rem(x + nx - j, nx)
            remote(gat.at[1 - c, xx], gat.at[1 - c, xx], wc_s.at[j], wc_r.at[j], sibling).wait_recv()

        def lay(zz):
            for xx in range(nx):
                for cc in range(2):
                    at_row = 8 * xx + 4 * cc
                    tmp[at_row:at_row + 4, :] = gat[cc, xx, zz].astype(F32)
            n = 8 * nx
            w[pl.ds(pl.multiple_of(zz * n, n), n), :] = tmp[...].astype(BF16)
        loop(nz, lay)

    def w_drain():
        loop(nz - 1, lambda j: wz(j).wait_send())
        for j in range(nx - 1):
            wx(j).wait_send()
        for j in range(nx):
            wc(j).wait_send()

    tile = min(256, piece)

    def w_cols(k):
        owner = lax.rem(y + k, ny)
        return w[:, pl.ds(pl.multiple_of(owner * 128, 128), 128)]

    def partial(*ks):
        def body(i):
            span = pl.ds(pl.multiple_of(i * tile, tile), tile)
            rhs = jnp.concatenate([w_cols(k) for k in ks], axis=1)
            out = jnp.dot(tok[span, :], rhs, preferred_element_type=F32)
            for n, k in enumerate(ks):
                part[k, span, :] = out[:, n * 128:(n + 1) * 128]
        loop(rows // tile, body)

    def rs(d, t, p):
        span = pl.ds(pl.multiple_of(p * piece, piece), piece)
        return remote(rss.at[d, t - 1, span], rsr.at[d, t - 1, span], rs_s.at[d, t - 1, p], rs_r.at[d, t - 1, p],
                      right if d == 0 else left)

    def rs_send(d, t, p, arrives):
        s = hops - t + 1
        k = s if d == 0 else ny - s
        span = pl.ds(pl.multiple_of(p * piece, piece), piece)
        total = part[k, span, :]
        if arrives:
            rs(d, t - 1, p).wait_recv()
            total = total + rsr[d, t - 2, span, :].astype(F32)
        rss[d, t - 1, span, :] = total.astype(BF16)
        rs(d, t, p).start()

    def rs_first():
        loop(half, lambda p: (rs_send(0, 1, p, False), rs_send(1, 1, p + half, False)))

    def rs_second_own():
        loop(half, lambda p: (rs_send(0, 2, p + half, False), rs_send(1, 2, p, False)))

    def rs_second_sum():
        loop(half, lambda p: (rs_send(0, 2, p, True), rs_send(1, 2, p + half, True)))

    def rs_step(t, late):
        def body(i):
            rs_send(0, t, i + (0 if late else half), True)
            rs_send(1, t, i + (half if late else 0), True)
        loop(half, body)

    def rs_last():
        def seen(i):
            rs(0, hops, i + half).wait_recv()
            rs(1, hops, i).wait_recv()
        loop(half, seen)

        def fin(i):
            a, b = i, i + half
            rs(0, hops, a).wait_recv()
            rs(1, hops, b).wait_recv()
            for p in (a, b):
                span = pl.ds(pl.multiple_of(p * piece, piece), piece)
                total = part[0, span, :] + rsr[0, hops - 1, span, :].astype(F32) + rsr[1, hops - 1, span, :].astype(F32)
                vout[span, :] = total.astype(BF16)
        loop(half, fin)

    def rs_drain():
        loop(half, lambda p: (rs(0, 1, p).wait_send(), rs(1, 1, p + half).wait_send()))
        for t in range(2, hops + 1):
            loop(PIECES, lambda p: (rs(0, t, p).wait_send(), rs(1, t, p).wait_send()))

    def token_grad(lo, hi):
        def body(i):
            span = pl.ds(pl.multiple_of((i + lo) * tile, tile), tile)
            lhs = jnp.concatenate([full[lax.rem(y + ny - k, ny), span, :] for k in range(ny)], axis=1)
            out = lax.dot_general(lhs, w[...], (((1,), (1,)), ((), ())), preferred_element_type=F32)
            tgout[span, :] = out.astype(BF16)
        loop(hi - lo, body)

    order = [0]
    for k in range(1, hops):
        order += [k, ny - k]
    order.append(hops)

    def slots(ph, cc):
        mb, start = sizes[ph], 2 * sum(sizes[:ph])
        first, second = order[start:start + mb], order[start + mb:start + 2 * mb]
        return [jnp.where(cc == 0, a, b) for a, b in zip(first, second)]

    def wg_term(ph, cc, out):
        group, mb = min(128, feats), sizes[ph]
        per = group // (8 * nx)

        def body(i):
            rhs = jnp.concatenate([full[s] for s in slots(ph, cc)], axis=1)
            term = jnp.dot(tok_t[pl.ds(pl.multiple_of(i * group, group), group), :], rhs, preferred_element_type=F32)
            for u in range(per):
                for xx in range(nx):
                    for m in range(mb):
                        lo = (u * nx + xx) * 8
                        out[ph][xx, i * per + u, m] = term[lo:lo + 8, m * 128:(m + 1) * 128].astype(out[ph].dtype)
        loop(feats // group, body)

    def gc(ph):
        return remote(sibs[ph], sibr[ph], gc_s.at[ph], gc_r.at[ph], sibling)

    def gx(ph, j):
        return remote(xs[ph].at[j], xr[ph].at[j], gx_s.at[ph, j], gx_r.at[ph, j], at(z, lax.rem(x + j + 1, nx), c))

    def gz(ph, j):
        zz = lax.rem(z + j + 1, nz)
        return remote(zs[ph].at[zz], zr[ph].at[j], gz_s.at[ph, j], gz_r.at[ph, j], at(zz, x, c))

    def gf(ph):
        return remote(fs[ph], fr[ph], gf_s.at[ph], gf_r.at[ph], sibling)

    def wg_theirs(ph):
        wg_term(ph, 1 - c, sibs)
        gc(ph).start()

    def wg_mine(ph):
        wg_term(ph, c, mine)

    def wg_along_x(ph):
        gc(ph).wait_recv()

        def body(zz):
            for j in range(nx):
                xx = lax.rem(x + j, nx)
                total = mine[ph][xx, zz] + sibr[ph][xx, zz].astype(F32)
                if j == 0:
                    mine[ph][xx, zz] = total
                else:
                    xs[ph][j - 1, zz] = total.astype(BF16)
        loop(nz, body)
        for j in range(nx - 1):
            gx(ph, j).start()

    def wg_along_z(ph):
        for j in range(nx - 1):
            gx(ph, j).wait_recv()

        def body(zz):
            total = mine[ph][x, zz]
            for j in range(nx - 1):
                total = total + xr[ph][j, zz].astype(F32)
            mine[ph][x, zz] = total
            zs[ph][zz] = total.astype(BF16)
        loop(nz, body)
        far_first(lambda j: gz(ph, j).start())

    def place(ph, cc, value):
        for m, s in enumerate(slots(ph, cc)):
            col = lax.rem(y + ny - s, ny) * 128
            wgout[:, pl.ds(pl.multiple_of(col, 128), 128)] = value[m]

    def wg_across(ph):
        loop(nz - 1, lambda j: gz(ph, j).wait_recv())
        total = mine[ph][x, z]
        for j in range(nz - 1):
            total = total + zr[ph][j].astype(F32)
        total = total * F32(inv)
        low, high = total[:, :4, :], total[:, 4:, :]
        fs[ph][...] = jnp.where(c == 0, high, low)
        gf(ph).start()
        place(ph, c, jnp.where(c == 0, low, high))

    def wg_last():
        for ph in range(2):
            gf(ph).wait_recv()
            place(ph, 1 - c, fr[ph][...])

    def wg_drain():
        for ph in range(2):
            gc(ph).wait_send()
            for j in range(nx - 1):
                gx(ph, j).wait_send()
            loop(nz - 1, lambda j: gz(ph, j).wait_send())
            gf(ph).wait_send()

    def turn():
        step = min(256, rows)

        def body(i):
            span = pl.ds(pl.multiple_of(i * step, step), step)
            tok_t[:, span] = tok[span, :].T
        loop(rows // step, body)

    cp_cot.wait()
    ag_first()
    cp_code.wait()
    cp_scale.wait()
    w_first()
    cp_tok.wait()
    turn()
    ag_hop(1)
    w_along_x()
    for h in range(2, hops - 1):
        ag_hop(h)
    wg_theirs(0)
    wg_mine(0)
    w_across()
    ag_hop(hops - 1)
    w_done()
    partial(hops)
    rs_first()
    wg_along_x(0)
    ag_hop(hops)
    wg_theirs(1)
    wg_mine(1)
    partial(hops - 1, hops + 1)
    rs_second_own()
    wg_along_x(1)
    rs_second_sum()
    wg_along_z(0)
    partial(2, ny - 2)
    rs_step(3, False)
    wg_along_z(1)
    partial(1, ny - 1)
    rs_step(3, True)
    wg_across(0)
    rs_step(4, False)
    partial(0)
    token_grad(0, rows // tile // 2)
    rs_step(4, True)
    token_grad(rows // tile // 2, rows // tile)
    wg_across(1)
    rs_last()
    wg_last()
    ag_drain()
    w_drain()
    wg_drain()
    rs_drain()


def deliver(a, b, d, a_out, b_out, d_out, sem):
    half = b.shape[0] // 2
    top, low = pl.ds(0, half), pl.ds(half, half)
    pairs = ((b.at[top], b_out.at[top]), (b.at[low], b_out.at[low]), (a, a_out), (d, d_out))
    copies = [pltpu.make_async_copy(src, dst, sem.at[i]) for i, (src, dst) in enumerate(pairs)]
    for cp in copies:
        cp.start()
    for cp in copies:
        cp.wait()


def on_device(ny, nz, nx, tokens, codes, scales, cot):
    rows, feats = tokens.shape
    cols = codes.shape[1]
    hops = ny // 2
    hbm = pl.BlockSpec(memory_space=pltpu.HBM)
    dma = pltpu.SemaphoreType.DMA
    v = pltpu.VMEM
    scratch = [
        v((rows, feats), BF16), v((feats, rows), BF16), v(codes.shape, BF16), v(scales.shape, BF16),
        v((ny, rows, 128), BF16), v((2, nx, nz, 4, cols), BF16), v((8 * nx, cols), F32), v((feats, cols), BF16),
        v((ny, rows, 128), F32), v((2, hops, rows, 128), BF16), v((2, hops, rows, 128), BF16),
        *(shape for mb in phases(ny) for shape in (
            v((nx, nz, mb, 8, 128), F32), v((nx, nz, mb, 8, 128), BF16), v((nx, nz, mb, 8, 128), BF16),
            v((nx - 1, nz, mb, 8, 128), BF16), v((nx - 1, nz, mb, 8, 128), BF16),
            v((nz, mb, 8, 128), BF16), v((nz - 1, mb, 8, 128), BF16),
            v((mb, 4, 128), F32), v((mb, 4, 128), F32))),
        dma((4,)),
        dma((2, hops, PIECES)), dma((2, hops, PIECES)), dma((2, hops, PIECES)), dma((2, hops, PIECES)),
        dma((nz - 1,)), dma((nz - 1,)), dma((nx - 1,)), dma((nx - 1,)), dma((nx,)), dma((nx,)),
        dma((2,)), dma((2,)), dma((2, nx - 1)), dma((2, nx - 1)), dma((2, nz - 1)), dma((2, nz - 1)),
        dma((2,)), dma((2,)),
    ]
    flops = 6 * rows * feats * cols
    shapes = (((rows, 128), BF16), ((rows, feats), BF16), ((4, cols), F32))
    results = pl.pallas_call(
        functools.partial(kernel, ny, nz, nx),
        out_shape=tuple(v(shape, dtype) for shape, dtype in shapes),
        in_specs=[hbm] * 4,
        out_specs=(pl.BlockSpec(memory_space=v),) * 3,
        scratch_shapes=scratch,
        compiler_params=pltpu.CompilerParams(
            collective_id=0, has_side_effects=True, vmem_limit_bytes=61 * 2**20),
        cost_estimate=pl.CostEstimate(flops=flops, bytes_accessed=4 * rows * feats, transcendentals=0),
    )(tokens, codes, scales, cot)
    return pl.pallas_call(
        deliver,
        out_shape=tuple(jax.ShapeDtypeStruct(shape, dtype) for shape, dtype in shapes),
        in_specs=[pl.BlockSpec(memory_space=v)] * 3,
        out_specs=(hbm,) * 3,
        scratch_shapes=[dma((4,))],
        compiler_params=pltpu.CompilerParams(vmem_limit_bytes=2**20),
        cost_estimate=pl.CostEstimate(flops=0, bytes_accessed=4 * rows * feats, transcendentals=0),
    )(*(pltpu.with_memory_space_constraint(r, v) for r in results))

def build(mesh, nx):
    ny = mesh.shape["node"]
    nz = mesh.shape["dp"] // (2 * nx)
    placed = (P("dp", "node"), P(("node", "dp"), None), P(("node", "dp"), None), P("dp", "node"))
    return jax.shard_map(
        functools.partial(on_device, ny, nz, nx),
        mesh=mesh,
        in_specs=placed,
        out_specs=(P("dp", "node"), P("dp", "node"), P(("node", "dp"), None)),
        check_vma=False,
    )


def solution(mesh):
    return build(mesh, NX)
```

```python
import functools
import math

import jax
import jax.numpy as jnp
from jax import lax
from jax.experimental import pallas as pl
from jax.experimental.pallas import tpu as pltpu
from jax.sharding import PartitionSpec as P

NX = 4
PIECES = 4
BF16, F32 = jnp.bfloat16, jnp.float32
MESH = pl.DeviceIdType.MESH


def phases(ny):
    return ny // 4, ny // 4


def kernel(ny, nz, nx, tok_ref, code_ref, scale_ref, cot_ref,
           vout, tgout, wgout,
           tok, tok_t, codes, scales, full, gat, tmp, w, part, rss, rsr,
           mine0, sibs0, sibr0, xs0, xr0, zs0, zr0, fs0, fr0, mine1, sibs1, sibr1, xs1, xr1, zs1, zr1, fs1, fr1,
           in_sem, ag_s, ag_r, rs_s, rs_r,
           wz_s, wz_r, wx_s, wx_r, wc_s, wc_r,
           gc_s, gc_r, gx_s, gx_r, gz_s, gz_r, gf_s, gf_r):
    rows, feats = tok.shape
    cols = codes.shape[1]
    hops = ny // 2
    piece = rows // PIECES
    half = PIECES // 2
    sizes = phases(ny)
    mine, sibs, sibr, xs, xr = (mine0, mine1), (sibs0, sibs1), (sibr0, sibr1), (xs0, xs1), (xr0, xr1)
    zs, zr, fs, fr = (zs0, zs1), (zr0, zr1), (fs0, fs1), (fr0, fr1)
    inv = 1.0 / math.sqrt(rows * nz * nx * 2)

    y = lax.axis_index("node")
    dp = lax.axis_index("dp")
    c = lax.rem(dp, 2)
    x = lax.rem(dp // 2, nx)
    z = dp // (2 * nx)

    def at(zz, xx, cc):
        return ((zz * nx + xx) * 2 + cc, y)

    right, left = (dp, lax.rem(y + 1, ny)), (dp, lax.rem(y + ny - 1, ny))
    sibling = at(z, x, 1 - c)

    def remote(src, dst, s_sem, r_sem, dev):
        return pltpu.make_async_remote_copy(
            src_ref=src, dst_ref=dst, send_sem=s_sem, recv_sem=r_sem, device_id=dev, device_id_type=MESH)

    def loop(n, body):
        lax.fori_loop(0, n, lambda i, carry: (body(i), carry)[1], 0)

    def far_first(body):
        def one(k):
            near = (k + 1) // 2
            body(nz // 2 - 1 + jnp.where(lax.rem(k, 2) == 0, near, -near))
        loop(nz - 1, one)

    cp_cot = pltpu.make_async_copy(cot_ref, full.at[0], in_sem.at[0])
    cp_code = pltpu.make_async_copy(code_ref, codes, in_sem.at[1])
    cp_scale = pltpu.make_async_copy(scale_ref, scales, in_sem.at[2])
    cp_tok = pltpu.make_async_copy(tok_ref, tok, in_sem.at[3])
    for cp in (cp_cot, cp_code, cp_scale, cp_tok):
        cp.start()

    barrier = pltpu.get_barrier_semaphore()

    def greet(dev):
        pl.semaphore_signal(barrier, inc=1, device_id=dev, device_id_type=MESH)

    greet(right)
    greet(left)
    greet(sibling)
    for j in range(1, nx):
        greet(at(z, lax.rem(x + j, nx), c))
    far_first(lambda j: greet(at(lax.rem(z + j + 1, nz), x, c)))
    pl.semaphore_wait(barrier, 3 + nx - 1 + nz - 1)

    def ag(d, h, p):
        src, dst = (h - 1, h) if d == 0 else ((ny - h + 1) % ny, ny - h)
        span = pl.ds(pl.multiple_of(p * piece, piece), piece)
        return remote(full.at[src, span], full.at[dst, span], ag_s.at[d, h - 1, p], ag_r.at[d, h - 1, p],
                      right if d == 0 else left)

    def ag_first():
        loop(PIECES, lambda p: (ag(0, 1, p).start(), ag(1, 1, p).start()))

    def ag_hop(h):
        if h == hops:
            loop(half, lambda p: (ag(0, h, p).wait_recv(), ag(1, h, p + half).wait_recv()))
        elif h == hops - 1:
            def body(p):
                q = p + half
                ag(0, h, p).wait_recv()
                ag(0, h + 1, p).start()
                ag(1, h, q).wait_recv()
                ag(1, h + 1, q).start()
            loop(half, body)
            loop(half, lambda p: (ag(0, h, p + half).wait_recv(), ag(1, h, p).wait_recv()))
        else:
            def body(p):
                ag(0, h, p).wait_recv()
                ag(0, h + 1, p).start()
                ag(1, h, p).wait_recv()
                ag(1, h + 1, p).start()
            loop(PIECES, body)

    def ag_drain():
        for h in range(1, hops):
            loop(PIECES, lambda p: (ag(0, h, p).wait_send(), ag(1, h, p).wait_send()))
        loop(half, lambda p: (ag(0, hops, p).wait_send(), ag(1, hops, p + half).wait_send()))

    def wz(j):
        return remote(gat.at[c, x, z], gat.at[c, x, z], wz_s.at[j], wz_r.at[j],
                      at(lax.rem(z + j + 1, nz), x, c))

    def wx(j):
        return remote(gat.at[c, x], gat.at[c, x], wx_s.at[j], wx_r.at[j], at(z, lax.rem(x + j + 1, nx), c))

    def wc(j):
        xx = lax.rem(x - j + nx, nx)
        return remote(gat.at[c, xx], gat.at[c, xx], wc_s.at[j], wc_r.at[j], sibling)

    def w_first():
        scale = scales[...].astype(F32)
        block = cols // scale.shape[1]
        for b in range(scale.shape[1]):
            span = slice(b * block, (b + 1) * block)
            gat[c, x, z, :, span] = (codes[:, span].astype(F32) * scale[:, b:b + 1]).astype(BF16)
        far_first(lambda j: wz(j).start())

    def w_along_x():
        def arrived(j):
            zz = lax.rem(z + nz - j - 1, nz)
            remote(gat.at[c, x, zz], gat.at[c, x, zz], wz_s.at[j], wz_r.at[j], sibling).wait_recv()
        loop(nz - 1, arrived)
        for j in (1, 0, 2):
            wx(j).start()
        wc(0).start()

    def w_across():
        for j in range(1, nx):
            xx = lax.rem(x + nx - j, nx)
            remote(gat.at[c, xx], gat.at[c, xx], wx_s.at[j - 1], wx_r.at[j - 1], sibling).wait_recv()
            wc(j).start()

    def w_done():
        for j in range(nx):
            xx = lax.rem(x + nx - j, nx)
            remote(gat.at[1 - c, xx], gat.at[1 - c, xx], wc_s.at[j], wc_r.at[j], sibling).wait_recv()

        def lay(zz):
            for xx in range(nx):
                for cc in range(2):
                    at_row = 8 * xx + 4 * cc
                    tmp[at_row:at_row + 4, :] = gat[cc, xx, zz].astype(F32)
            n = 8 * nx
            w[pl.ds(pl.multiple_of(zz * n, n), n), :] = tmp[...].astype(BF16)
        loop(nz, lay)

    def w_drain():
        loop(nz - 1, lambda j: wz(j).wait_send())
        for j in range(nx - 1):
            wx(j).wait_send()
        for j in range(nx):
            wc(j).wait_send()

    tile = min(256, piece)

    def w_cols(k):
        owner = lax.rem(y + k, ny)
        return w[:, pl.ds(pl.multiple_of(owner * 128, 128), 128)]

    def partial(*ks):
        def body(i):
            span = pl.ds(pl.multiple_of(i * tile, tile), tile)
            rhs = jnp.concatenate([w_cols(k) for k in ks], axis=1)
            out = jnp.dot(tok[span, :], rhs, preferred_element_type=F32)
            for n, k in enumerate(ks):
                part[k, span, :] = out[:, n * 128:(n + 1) * 128]
        loop(rows // tile, body)

    def rs(d, t, p):
        span = pl.ds(pl.multiple_of(p * piece, piece), piece)
        return remote(rss.at[d, t - 1, span], rsr.at[d, t - 1, span], rs_s.at[d, t - 1, p], rs_r.at[d, t - 1, p],
                      right if d == 0 else left)

    def rs_send(d, t, p, arrives):
        s = hops - t + 1
        k = s if d == 0 else ny - s
        span = pl.ds(pl.multiple_of(p * piece, piece), piece)
        total = part[k, span, :]
        if arrives:
            rs(d, t - 1, p).wait_recv()
            total = total + rsr[d, t - 2, span, :].astype(F32)
        rss[d, t - 1, span, :] = total.astype(BF16)
        rs(d, t, p).start()

    def rs_first():
        loop(half, lambda p: (rs_send(0, 1, p, False), rs_send(1, 1, p + half, False)))

    def rs_second_own():
        loop(half, lambda p: (rs_send(0, 2, p + half, False), rs_send(1, 2, p, False)))

    def rs_second_sum():
        loop(half, lambda p: (rs_send(0, 2, p, True), rs_send(1, 2, p + half, True)))

    def rs_step(t, late):
        def body(i):
            rs_send(0, t, i + (0 if late else half), True)
            rs_send(1, t, i + (half if late else 0), True)
        loop(half, body)

    def rs_last():
        def seen(i):
            rs(0, hops, i + half).wait_recv()
            rs(1, hops, i).wait_recv()
        loop(half, seen)

        def fin(i):
            a, b = i, i + half
            rs(0, hops, a).wait_recv()
            rs(1, hops, b).wait_recv()
            for p in (a, b):
                span = pl.ds(pl.multiple_of(p * piece, piece), piece)
                total = part[0, span, :] + rsr[0, hops - 1, span, :].astype(F32) + rsr[1, hops - 1, span, :].astype(F32)
                vout[span, :] = total.astype(BF16)
        loop(half, fin)

    def rs_drain():
        loop(half, lambda p: (rs(0, 1, p).wait_send(), rs(1, 1, p + half).wait_send()))
        for t in range(2, hops + 1):
            loop(PIECES, lambda p: (rs(0, t, p).wait_send(), rs(1, t, p).wait_send()))

    def token_grad(lo, hi):
        def body(i):
            span = pl.ds(pl.multiple_of((i + lo) * tile, tile), tile)
            lhs = jnp.concatenate([full[lax.rem(y + ny - k, ny), span, :] for k in range(ny)], axis=1)
            out = lax.dot_general(lhs, w[...], (((1,), (1,)), ((), ())), preferred_element_type=F32)
            tgout[span, :] = out.astype(BF16)
        loop(hi - lo, body)

    order = [0]
    for k in range(1, hops):
        order += [k, ny - k]
    order.append(hops)

    def slots(ph, cc):
        mb, start = sizes[ph], 2 * sum(sizes[:ph])
        first, second = order[start:start + mb], order[start + mb:start + 2 * mb]
        return [jnp.where(cc == 0, a, b) for a, b in zip(first, second)]

    def wg_term(ph, cc, out):
        group, mb = min(128, feats), sizes[ph]
        per = group // (8 * nx)

        def body(i):
            rhs = jnp.concatenate([full[s] for s in slots(ph, cc)], axis=1)
            term = jnp.dot(tok_t[pl.ds(pl.multiple_of(i * group, group), group), :], rhs, preferred_element_type=F32)
            for u in range(per):
                for xx in range(nx):
                    for m in range(mb):
                        lo = (u * nx + xx) * 8
                        out[ph][xx, i * per + u, m] = term[lo:lo + 8, m * 128:(m + 1) * 128].astype(out[ph].dtype)
        loop(feats // group, body)

    def gc(ph):
        return remote(sibs[ph], sibr[ph], gc_s.at[ph], gc_r.at[ph], sibling)

    def gx(ph, j):
        return remote(xs[ph].at[j], xr[ph].at[j], gx_s.at[ph, j], gx_r.at[ph, j], at(z, lax.rem(x + j + 1, nx), c))

    def gz(ph, j):
        zz = lax.rem(z + j + 1, nz)
        return remote(zs[ph].at[zz], zr[ph].at[j], gz_s.at[ph, j], gz_r.at[ph, j], at(zz, x, c))

    def gf(ph):
        return remote(fs[ph], fr[ph], gf_s.at[ph], gf_r.at[ph], sibling)

    def wg_theirs(ph):
        wg_term(ph, 1 - c, sibs)
        gc(ph).start()

    def wg_mine(ph):
        wg_term(ph, c, mine)

    def wg_along_x(ph):
        gc(ph).wait_recv()

        def body(zz):
            for j in range(nx):
                xx = lax.rem(x + j, nx)
                total = mine[ph][xx, zz] + sibr[ph][xx, zz].astype(F32)
                if j == 0:
                    mine[ph][xx, zz] = total
                else:
                    xs[ph][j - 1, zz] = total.astype(BF16)
        loop(nz, body)
        for j in (1, 0, 2):
            gx(ph, j).start()

    def wg_along_z(ph):
        for j in range(nx - 1):
            gx(ph, j).wait_recv()

        def body(zz):
            total = mine[ph][x, zz]
            for j in range(nx - 1):
                total = total + xr[ph][j, zz].astype(F32)
            mine[ph][x, zz] = total
            zs[ph][zz] = total.astype(BF16)
        loop(nz, body)
        far_first(lambda j: gz(ph, j).start())

    def place(ph, cc, value):
        for m, s in enumerate(slots(ph, cc)):
            col = lax.rem(y + ny - s, ny) * 128
            wgout[:, pl.ds(pl.multiple_of(col, 128), 128)] = value[m]

    def wg_across(ph):
        loop(nz - 1, lambda j: gz(ph, j).wait_recv())
        total = mine[ph][x, z]
        for j in range(nz - 1):
            total = total + zr[ph][j].astype(F32)
        total = total * F32(inv)
        low, high = total[:, :4, :], total[:, 4:, :]
        fs[ph][...] = jnp.where(c == 0, high, low)
        gf(ph).start()
        place(ph, c, jnp.where(c == 0, low, high))

    def wg_last():
        for ph in range(2):
            gf(ph).wait_recv()
            place(ph, 1 - c, fr[ph][...])

    def wg_drain():
        for ph in range(2):
            gc(ph).wait_send()
            for j in range(nx - 1):
                gx(ph, j).wait_send()
            loop(nz - 1, lambda j: gz(ph, j).wait_send())
            gf(ph).wait_send()

    def turn():
        step = min(256, rows)

        def body(i):
            span = pl.ds(pl.multiple_of(i * step, step), step)
            tok_t[:, span] = tok[span, :].T
        loop(rows // step, body)

    cp_cot.wait()
    ag_first()
    cp_code.wait()
    cp_scale.wait()
    w_first()
    ag_hop(1)
    w_along_x()
    cp_tok.wait()
    turn()
    for h in range(2, hops - 1):
        ag_hop(h)
    wg_theirs(0)
    wg_mine(0)
    w_across()
    ag_hop(hops - 1)
    w_done()
    partial(hops)
    rs_first()
    wg_along_x(0)
    ag_hop(hops)
    wg_theirs(1)
    wg_mine(1)
    partial(hops - 1, hops + 1)
    rs_second_own()
    wg_along_x(1)
    rs_second_sum()
    wg_along_z(0)
    partial(2, ny - 2)
    rs_step(3, False)
    wg_along_z(1)
    partial(1, ny - 1)
    rs_step(3, True)
    wg_across(0)
    rs_step(4, False)
    partial(0)
    token_grad(0, rows // tile // 2)
    rs_step(4, True)
    token_grad(rows // tile // 2, rows // tile)
    wg_across(1)
    rs_last()
    wg_last()
    ag_drain()
    w_drain()
    wg_drain()
    rs_drain()


def deliver(a, b, d, a_out, b_out, d_out, sem):
    half = b.shape[0] // 2
    top, low = pl.ds(0, half), pl.ds(half, half)
    pairs = ((b.at[top], b_out.at[top]), (b.at[low], b_out.at[low]), (a, a_out), (d, d_out))
    copies = [pltpu.make_async_copy(src, dst, sem.at[i]) for i, (src, dst) in enumerate(pairs)]
    for cp in copies:
        cp.start()
    for cp in copies:
        cp.wait()


def on_device(ny, nz, nx, tokens, codes, scales, cot):
    rows, feats = tokens.shape
    cols = codes.shape[1]
    hops = ny // 2
    hbm = pl.BlockSpec(memory_space=pltpu.HBM)
    dma = pltpu.SemaphoreType.DMA
    v = pltpu.VMEM
    scratch = [
        v((rows, feats), BF16), v((feats, rows), BF16), v(codes.shape, BF16), v(scales.shape, BF16),
        v((ny, rows, 128), BF16), v((2, nx, nz, 4, cols), BF16), v((8 * nx, cols), F32), v((feats, cols), BF16),
        v((ny, rows, 128), F32), v((2, hops, rows, 128), BF16), v((2, hops, rows, 128), BF16),
        *(shape for mb in phases(ny) for shape in (
            v((nx, nz, mb, 8, 128), F32), v((nx, nz, mb, 8, 128), BF16), v((nx, nz, mb, 8, 128), BF16),
            v((nx - 1, nz, mb, 8, 128), BF16), v((nx - 1, nz, mb, 8, 128), BF16),
            v((nz, mb, 8, 128), BF16), v((nz - 1, mb, 8, 128), BF16),
            v((mb, 4, 128), F32), v((mb, 4, 128), F32))),
        dma((4,)),
        dma((2, hops, PIECES)), dma((2, hops, PIECES)), dma((2, hops, PIECES)), dma((2, hops, PIECES)),
        dma((nz - 1,)), dma((nz - 1,)), dma((nx - 1,)), dma((nx - 1,)), dma((nx,)), dma((nx,)),
        dma((2,)), dma((2,)), dma((2, nx - 1)), dma((2, nx - 1)), dma((2, nz - 1)), dma((2, nz - 1)),
        dma((2,)), dma((2,)),
    ]
    flops = 6 * rows * feats * cols
    shapes = (((rows, 128), BF16), ((rows, feats), BF16), ((4, cols), F32))
    results = pl.pallas_call(
        functools.partial(kernel, ny, nz, nx),
        out_shape=tuple(v(shape, dtype) for shape, dtype in shapes),
        in_specs=[hbm] * 4,
        out_specs=(pl.BlockSpec(memory_space=v),) * 3,
        scratch_shapes=scratch,
        compiler_params=pltpu.CompilerParams(
            collective_id=0, has_side_effects=True, vmem_limit_bytes=61 * 2**20),
        cost_estimate=pl.CostEstimate(flops=flops, bytes_accessed=4 * rows * feats, transcendentals=0),
    )(tokens, codes, scales, cot)
    return pl.pallas_call(
        deliver,
        out_shape=tuple(jax.ShapeDtypeStruct(shape, dtype) for shape, dtype in shapes),
        in_specs=[pl.BlockSpec(memory_space=v)] * 3,
        out_specs=(hbm,) * 3,
        scratch_shapes=[dma((4,))],
        compiler_params=pltpu.CompilerParams(vmem_limit_bytes=2**20),
        cost_estimate=pl.CostEstimate(flops=0, bytes_accessed=4 * rows * feats, transcendentals=0),
    )(*(pltpu.with_memory_space_constraint(r, v) for r in results))

def build(mesh, nx):
    ny = mesh.shape["node"]
    nz = mesh.shape["dp"] // (2 * nx)
    placed = (P("dp", "node"), P(("node", "dp"), None), P(("node", "dp"), None), P("dp", "node"))
    return jax.shard_map(
        functools.partial(on_device, ny, nz, nx),
        mesh=mesh,
        in_specs=placed,
        out_specs=(P("dp", "node"), P("dp", "node"), P(("node", "dp"), None)),
        check_vma=False,
    )


def solution(mesh):
    return build(mesh, NX)
```
